32 devices in a mesh: groups: 2 (over y), page: 4 (over z), tensor: 4 (over x, core).
Axes of the slice: x: 2, y: 2, z: 4, core: 2. Of those that a mesh axis runs over, the one named last changes fastest.
Arguments:
- query: bfloat16 [4096, 4096], P(('groups', 'page'), 'tensor'), parts along dimension 0, may hold values from -13 to 13
- memory: bfloat16 [2048, 1024], P(('groups', 'page'), 'tensor'), parts along dimension 0, may hold values from -20 to 20
- key_weight: bfloat16 [1024, 4096], P(None, 'tensor'), may hold values from -2.6 to 2.6
- value_weight: bfloat16 [1024, 4096], P(None, 'tensor'), may hold values from -0.1875 to 0.1875
- out_grad: bfloat16 [4096, 4096], P(('groups', 'page'), 'tensor'), parts along dimension 0, may hold values from -6 to 6
- mask_blocks: int32 [8, 3, 4, 2], P(('groups', 'page')), parts along dimension 0, may hold values from 0 to 1, as said below
Outputs:
- attended: bfloat16 [4096, 4096], P(('groups', 'page'), 'tensor'), parts along dimension 0
- query_grad: bfloat16 [4096, 4096], P(('groups', 'page'), 'tensor'), parts along dimension 0
- memory_grad: bfloat16 [2048, 1024], P(('groups', 'page'), 'tensor'), parts along dimension 0
The draws below stay inside these ranges and needn't reach their ends.
There are 2 independent parts, one for each index of `groups`. The reference program is written for one: setup_inputs(seed, part) draws one part's arguments, and reference() takes and returns one part's arrays. A program takes and returns all parts, laid end to end along the dimension named above; an argument that names none is the same for every part. Nothing has to cross between parts.
Inputs may be any that keep to these rules, and one draw needn't show every extreme that they name: `mask_blocks`: for every page and every block of 128 query rows, at least one block of the page's own memory (slot 1) is marked.
All inputs are finite; a program needn't handle non-finite values.
Results may differ from the reference program's by a relative error of at most 0.02.
The reference program's roundings to bfloat16 on the way (of `keys`, `values`, `rounded_weights`, `score_grad`, `key_piece` and `value_piece`) count: a program that leaves them out, or rounds other values in their place, can miss the bound.
Values may be sent and summed in bfloat16 or wider, within the bound.
A program may use at most 128 MiB of HBM per device.

```python
import math
import jax
import jax.numpy as jnp
from jax import lax

BLOCK = 128
HD = 128
HEADS = 32
DM = 1024
TOK = 512
MEM = 256
PAGES = 4
TOKENS = 2048
MEMROWS = 1024
FEAT = 4096
TB = 4
MB = 2


def draw_key_weight(key, part):
    matrix = jnp.clip(jax.random.normal(jax.random.fold_in(key, 11), (DM, FEAT), jnp.float32), -6.0, 6.0) * DM ** (-0.5)
    return matrix.astype(jnp.bfloat16)


def draw_memory(key, part):
    values = jnp.clip(jax.random.normal(jax.random.fold_in(key, 21), (MEMROWS, DM), jnp.float32), -6.0, 6.0)
    row_scale = jnp.exp(jax.random.uniform(jax.random.fold_in(key, 22), (MEMROWS, 1), jnp.float32, -1.15, 1.15))
    values = values * row_scale
    return values.astype(jnp.bfloat16)


def draw_query(key, part):
    values = jnp.clip(jax.random.normal(jax.random.fold_in(key, 41), (TOKENS, FEAT), jnp.float32), -6.0, 6.0)
    row_scale = jnp.exp(jax.random.uniform(jax.random.fold_in(key, 42), (TOKENS, 1), jnp.float32, -0.7, 0.7))
    values = values * row_scale
    return values.astype(jnp.bfloat16)


def draw_mask_blocks(key, part):
    random_bits = jax.random.randint(jax.random.fold_in(key, 31), (PAGES, 3, TB, MB), 0, 2, dtype=jnp.int32)
    chosen = jax.random.randint(jax.random.fold_in(key, 32), (PAGES, TB, 1), 0, MB, dtype=jnp.int32)
    own_forced = (jnp.arange(MB, dtype=jnp.int32)[None, None, :] == chosen).astype(jnp.int32)
    return random_bits.at[:, 1].set(jnp.maximum(random_bits[:, 1], own_forced))


def shard_levels(stream_key, dims, shards, smallest, high):
    def one(dim, blocks):
        heights = jax.random.uniform(jax.random.fold_in(jax.random.fold_in(stream_key, 6), dim), (blocks,), jnp.float32, smallest / len(shards), high / len(shards))
        return jnp.repeat(jnp.exp(heights), dims[dim] // blocks).reshape((-1,) + (1,) * (len(dims) - dim - 1))

    gain = one(*shards[0])
    for cut in shards[1:]:
        gain = gain * one(*cut)
    return gain


def noise(stream_key, shape, width, most, cuts=(), kind=jnp.bfloat16):
    array = jax.random.normal(stream_key, shape, jnp.float32) * width
    if len(cuts) > 0:
        array = shard_levels(stream_key, shape, cuts, -0.22, 0.18) * array
    return jnp.clip(array, min=-most, max=most).astype(kind)


def setup_inputs(seed: int = 0, part: int = 0) -> dict:
    key_of = jax.random.split(jax.random.key(seed), 7)
    part_keys = jax.random.split(jax.random.fold_in(key_of[6], part), 7)
    return {
        "query": draw_query(jax.random.fold_in(jax.random.fold_in(key_of[6], part), 71), part),
        "memory": draw_memory(jax.random.fold_in(jax.random.fold_in(key_of[6], part), 71), part),
        "key_weight": draw_key_weight(jax.random.fold_in(key_of[6], 71), part),
        "value_weight": noise(key_of[3], (DM, FEAT), DM ** -0.5, 0.1875, ((1, 4),)),
        "out_grad": noise(part_keys[4], (TOKENS, FEAT), 1.0, 6.0, ((0, 4), (1, 4))),
        "mask_blocks": draw_mask_blocks(jax.random.fold_in(jax.random.fold_in(key_of[6], part), 71), part),
    }


masked_score = -1e+30

def expand_mask(page_blocks, source_live):
    block_grid = page_blocks.astype(jnp.float32) * source_live[:, None, None]
    block_grid = jnp.repeat(jnp.repeat(block_grid, BLOCK, axis=1), BLOCK, axis=2)
    return jnp.transpose(block_grid, (1, 0, 2)).reshape(TOK, 3 * MEM)

def reference(query, memory, key_weight, value_weight, out_grad, mask_blocks):
    keys = jnp.dot(memory, key_weight, preferred_element_type=jnp.float32).astype(jnp.bfloat16)
    values = jnp.dot(memory, value_weight, preferred_element_type=jnp.float32).astype(jnp.bfloat16)
    zero_rows = jnp.zeros((MEM, FEAT), keys.dtype)
    keys_padded = jnp.concatenate([zero_rows, keys, zero_rows], 0)
    values_padded = jnp.concatenate([zero_rows, values, zero_rows], 0)
    score_scale = 1.0 / math.sqrt(HD)

    def one_page(page_index):
        mem_start = (page_index * MEM).astype(jnp.int32)
        tok_start = (page_index * TOK).astype(jnp.int32)
        key_slab = lax.dynamic_slice_in_dim(keys_padded, mem_start, 3 * MEM, 0)
        value_slab = lax.dynamic_slice_in_dim(values_padded, mem_start, 3 * MEM, 0)
        query_rows = lax.dynamic_slice_in_dim(query, tok_start, TOK, 0)
        grad_in = lax.dynamic_slice_in_dim(out_grad, tok_start, TOK, 0)
        sources = page_index + jnp.arange(3, dtype=jnp.int32) - 1
        source_live = ((sources >= 0) & (sources < PAGES)).astype(jnp.float32)
        visible = expand_mask(mask_blocks[page_index], source_live)
        query_heads = query_rows.reshape(TOK, HEADS, HD).astype(jnp.float32)
        key_heads = key_slab.reshape(3 * MEM, HEADS, HD).astype(jnp.float32)
        value_heads = value_slab.reshape(3 * MEM, HEADS, HD).astype(jnp.float32)
        scores = jnp.einsum('thd,khd->htk', query_heads, key_heads) * score_scale
        scores = jnp.where(visible[None] > 0, scores, masked_score)
        row_max = lax.optimization_barrier(jnp.max(scores, axis=2, keepdims=True))
        exponent = jnp.exp(scores - row_max)
        weights = exponent / lax.optimization_barrier(jnp.sum(exponent, axis=2, keepdims=True))
        rounded_weights = weights.astype(jnp.bfloat16).astype(jnp.float32)
        mixed = jnp.einsum('htk,khd->thd', rounded_weights, value_heads)
        attended = mixed.reshape(TOK, FEAT).astype(jnp.bfloat16)
        grad_rows = grad_in.astype(jnp.float32).reshape(TOK, HEADS, HD)
        weight_grad = jnp.einsum('thd,khd->htk', grad_rows, value_heads)
        row_inner = lax.optimization_barrier(jnp.sum(weights * weight_grad, axis=2, keepdims=True))
        score_grad = (weights * (weight_grad - row_inner) * score_scale).astype(jnp.bfloat16).astype(jnp.float32)
        query_grad = jnp.einsum('htk,khd->thd', score_grad, key_heads).reshape(TOK, FEAT).astype(jnp.bfloat16)
        key_piece = jnp.einsum('htk,thd->khd', score_grad, query_heads).reshape(3 * MEM, FEAT).astype(jnp.bfloat16)
        value_piece = jnp.einsum('htk,thd->khd', rounded_weights, grad_rows).reshape(3 * MEM, FEAT).astype(jnp.bfloat16)
        return (attended, query_grad, key_piece, value_piece)
    attended, query_grad, key_piece, value_piece = lax.map(one_page, jnp.arange(PAGES, dtype=jnp.int32))
    attended = attended.reshape(TOKENS, FEAT)
    query_grad = query_grad.reshape(TOKENS, FEAT)

    def aimed(pieces):
        zero_piece = jnp.zeros((1, MEM, FEAT), pieces.dtype)
        from_next = jnp.concatenate([pieces[1:, :MEM], zero_piece], 0)
        from_prev = jnp.concatenate([zero_piece, pieces[:-1, 2 * MEM:]], 0)
        own_part = pieces[:, MEM:2 * MEM]
        return [own_part.reshape(MEMROWS, FEAT), from_next.reshape(MEMROWS, FEAT), from_prev.reshape(MEMROWS, FEAT)]
    total = jnp.zeros((MEMROWS, DM), jnp.float32)
    for slot_keys, slot_values in zip(aimed(key_piece), aimed(value_piece)):
        total = total + jnp.dot(slot_keys, key_weight.T, preferred_element_type=jnp.float32)
        total = total + jnp.dot(slot_values, value_weight.T, preferred_element_type=jnp.float32)
    memory_grad = total.astype(jnp.bfloat16)
    return (attended, query_grad, memory_grad)
```

```python
import functools
import math

import jax
import jax.numpy as jnp
from jax import lax
from jax.experimental import pallas as pl
from jax.experimental.pallas import tpu as pltpu
from jax.sharding import PartitionSpec as P

HD = 128
MESH = pl.DeviceIdType.MESH
VMEM_LIMIT = 56 * 1024 * 1024
F32 = jnp.float32
BF16 = jnp.bfloat16


def place():
    page = lax.axis_index("page")
    tensor = lax.axis_index("tensor")
    core = lax.rem(tensor, 2)
    return page, tensor, core, tensor + 1 - 2 * core


def greet(pages, tensors):
    page, tensor, core, sibling = place()
    barrier = pltpu.get_barrier_semaphore()
    chips = tensors // 2

    def signal(where):
        pl.semaphore_signal(barrier, inc=1, device_id=where, device_id_type=MESH)

    signal({"tensor": sibling})
    for d in range(1, chips):
        signal({"tensor": lax.rem(tensor + 2 * d, tensors)})

    @pl.when(page > 0)
    def _():
        signal({"page": page - 1})

    @pl.when(page < pages - 1)
    def _():
        signal({"page": page + 1})

    def wait():
        at_end = jnp.where(page > 0, 1, 0) + jnp.where(page < pages - 1, 1, 0)
        pl.semaphore_wait(barrier, chips + at_end)

    return wait


def remote(src, dst, send, recv, where):
    return pltpu.make_async_remote_copy(
        src_ref=src, dst_ref=dst, send_sem=send, recv_sem=recv, device_id=where, device_id_type=MESH
    )


def project_kernel(
    pages, tensors, mem_ref, wk_hbm, wv_hbm, k_hbm, v_hbm,
    gathered, wk, wv, keys, values, load_sem, store_sem, send_sem, recv_sem,
):
    page, tensor, core, sibling = place()
    chips = tensors // 2
    rows, width = mem_ref.shape
    features = wk.shape[1]
    tile = min(256, features)

    loads = [
        pltpu.make_async_copy(wk_hbm, wk, load_sem.at[0]),
        pltpu.make_async_copy(wv_hbm, wv, load_sem.at[1]),
    ]
    wait_barrier = greet(pages, tensors)
    for load in loads:
        load.start()
    gathered[1, tensor] = mem_ref[...]
    has_prev = page > 0
    has_next = page < pages - 1

    def to_sibling(src, slot, owner):
        return remote(src, gathered.at[slot, owner], send_sem.at[slot, owner], recv_sem.at[slot, owner], {"tensor": sibling})

    def to_chip(src, d):
        there = lax.rem(tensor + 2 * d, tensors)
        return remote(src, gathered.at[1, tensor], send_sem.at[3, there], recv_sem.at[1, tensor], {"tensor": there})

    def to_next(src, owner):
        return remote(src, gathered.at[0, owner], send_sem.at[4, owner], recv_sem.at[0, owner], {"page": page + 1})

    def to_prev(src, owner):
        return remote(src, gathered.at[2, owner], send_sem.at[5, owner], recv_sem.at[2, owner], {"page": page - 1})

    def arrived(slot, owner):
        remote(
            gathered.at[slot, owner], gathered.at[slot, owner], send_sem.at[0, owner],
            recv_sem.at[slot, owner], {"tensor": sibling},
        ).wait_recv()

    def spread(src, owner):
        @pl.when(has_next)
        def _():
            to_next(src, owner).start()

        @pl.when(has_prev)
        def _():
            to_prev(src, owner).start()

    wait_barrier()
    for d in range(1, chips):
        to_chip(mem_ref, d).start()
    spread(mem_ref, tensor)
    to_sibling(mem_ref, 1, tensor).start()
    peers = [lax.rem(tensor + 2 * d, tensors) for d in range(chips)]
    for owner in peers[1:]:
        arrived(1, owner)
        spread(gathered.at[1, owner], owner)
        to_sibling(gathered.at[1, owner], 1, owner).start()

    stores = {}

    def project(slot):
        def step(i, _):
            columns = pl.ds(pl.multiple_of(i * tile, tile), tile)
            whole = jnp.concatenate([gathered[slot, owner] for owner in range(tensors)], axis=1)
            keys[slot, :, columns] = jnp.dot(whole, wk[:, columns], preferred_element_type=F32).astype(BF16)
            values[slot, :, columns] = jnp.dot(whole, wv[:, columns], preferred_element_type=F32).astype(BF16)
            return 0

        lax.fori_loop(0, features // tile, step, 0)

    def write(slot):
        span = pl.ds(slot * rows, rows)
        stores[slot] = [
            pltpu.make_async_copy(keys.at[slot], k_hbm.at[span], store_sem.at[slot, 0]),
            pltpu.make_async_copy(values.at[slot], v_hbm.at[span], store_sem.at[slot, 1]),
        ]
        for store in stores[slot]:
            store.start()

    def other(owner):
        return owner + 1 - 2 * lax.rem(owner, 2)

    def pass_on(k):
        @pl.when(has_prev)
        def _():
            arrived(0, peers[k])
            to_sibling(gathered.at[0, peers[k]], 0, peers[k]).start()

        @pl.when(has_next)
        def _():
            arrived(2, peers[k])
            to_sibling(gathered.at[2, peers[k]], 2, peers[k]).start()

    for owner in peers:
        arrived(1, other(owner))
    for load in loads:
        load.wait()
    project(1)
    write(1)
    for k in range(chips):
        pass_on(k)
    for slot, there in ((0, has_prev), (2, has_next)):
        @pl.when(there)
        def _():
            for owner in peers:
                arrived(slot, other(owner))
            project(slot)

        @pl.when(jnp.logical_not(there))
        def _():
            keys[slot] = jnp.zeros(keys.shape[1:], BF16)
            values[slot] = jnp.zeros(values.shape[1:], BF16)

        write(slot)

    for d in range(1, chips):
        to_chip(mem_ref, d).wait_send()
    for owner in peers:
        to_sibling(mem_ref, 1, owner).wait_send()

        @pl.when(has_next)
        def _():
            to_next(mem_ref, owner).wait_send()
            to_sibling(mem_ref, 2, owner).wait_send()

        @pl.when(has_prev)
        def _():
            to_prev(mem_ref, owner).wait_send()
            to_sibling(mem_ref, 0, owner).wait_send()
    for slot in (1, 0, 2):
        for store in stores[slot]:
            store.wait()


def attend_kernel(pages, mask_ref, q_ref, g_ref, k_ref, v_ref, att_ref, qg_ref, kp_ref, vp_ref):
    page = lax.axis_index("page")
    slots, query_blocks, memory_blocks = mask_ref.shape[1:]
    block = q_ref.shape[0] // query_blocks
    scale = 1.0 / math.sqrt(HD)
    rate = scale * math.log2(math.e)
    nt = (((1,), (1,)), ((), ()))
    tn = (((0,), (0,)), ((), ()))
    for head in range(q_ref.shape[1] // HD):
        cols = slice(head * HD, (head + 1) * HD)
        q, g, k, v = q_ref[:, cols], g_ref[:, cols], k_ref[:, cols], v_ref[:, cols]
        scores = lax.dot_general(k, q, nt, preferred_element_type=F32)
        weight_grad = lax.dot_general(v, g, nt, preferred_element_type=F32)
        rounded, score_grads = [], []
        for tb in range(query_blocks):
            span = slice(tb * block, (tb + 1) * block)
            parts = []
            for slot in range(slots):
                source = page + (slot - 1)
                live = jnp.logical_and(source >= 0, source < pages)
                for mb in range(memory_blocks):
                    seen = jnp.logical_and(mask_ref[0, slot, tb, mb] > 0, live)
                    low = (slot * memory_blocks + mb) * block
                    parts.append(scores[low : low + block, span] + jnp.where(seen, 0.0, -1e30).astype(F32))
            biased = jnp.concatenate(parts, axis=0)
            top = jnp.max(biased, axis=0, keepdims=True)
            exponent = jnp.exp2((biased - top) * rate)
            weights = exponent * (1.0 / jnp.sum(exponent, axis=0, keepdims=True))
            rounded.append(weights.astype(BF16))
            grad = weight_grad[:, span]
            inner = jnp.sum(weights * grad, axis=0, keepdims=True)
            score_grads.append((weights * (grad - inner)).astype(BF16))
        rounded = jnp.concatenate(rounded, axis=1)
        score_grad = jnp.concatenate(score_grads, axis=1)
        att = lax.dot_general(v, rounded, tn, preferred_element_type=F32)
        att_ref[:, cols] = att.T.astype(BF16)
        vp_ref[:, cols] = jnp.dot(rounded, g, preferred_element_type=F32).astype(BF16)
        qg = lax.dot_general(k, score_grad, tn, preferred_element_type=F32) * scale
        qg_ref[:, cols] = qg.T.astype(BF16)
        kp_ref[:, cols] = (jnp.dot(score_grad, q, preferred_element_type=F32) * scale).astype(BF16)


def reduce_kernel(
    pages, tensors, kp_hbm, vp_hbm, wk_hbm, wv_hbm, out_ref,
    kp, vp, wk, wv, own, stage, from_core, page_stage, from_page, chip_stage, from_chip,
    load_sem, core_send, core_recv, page_send, page_recv, chip_send, chip_recv,
):
    page, tensor, core, sibling = place()
    chips = tensors // 2
    chip = tensor // 2
    rows, width = out_ref.shape
    nt = (((1,), (1,)), ((), ()))
    wait_barrier = greet(pages, tensors)
    loads = [
        pltpu.make_async_copy(wk_hbm, wk, load_sem.at[0]),
        pltpu.make_async_copy(kp_hbm, kp, load_sem.at[1]),
        pltpu.make_async_copy(wv_hbm, wv, load_sem.at[2]),
        pltpu.make_async_copy(vp_hbm, vp, load_sem.at[3]),
    ]
    for load in loads:
        load.start()

    def partial(slot, group):
        take = pl.ds(pl.multiple_of(group * width, width), width)
        span = slice(slot * rows, (slot + 1) * rows)
        return lax.dot_general(kp[span], wk[take], nt, preferred_element_type=F32) + lax.dot_general(
            vp[span], wv[take], nt, preferred_element_type=F32
        )

    def to_core(slot, there):
        return remote(
            stage.at[slot, there], from_core.at[slot, there], core_send.at[slot, there],
            core_recv.at[slot, there], {"tensor": sibling},
        )

    def to_page(side, there):
        return remote(
            page_stage.at[side, there], from_page.at[side, there], page_send.at[side, there],
            page_recv.at[side, there], {"page": page - 1 + 2 * side},
        )

    def to_chip(there):
        return remote(
            chip_stage.at[there], from_chip.at[chip], chip_send.at[there], chip_recv.at[chip],
            {"tensor": 2 * there + core},
        )

    def chip_arrived(there):
        remote(
            chip_stage.at[there], from_chip.at[there], chip_send.at[there], chip_recv.at[there],
            {"tensor": 2 * there + core},
        ).wait_recv()

    order = [lax.rem(chip + 1 + k, chips) for k in range(chips)]

    def partials(slot, before_send=None):
        for there in order:
            stage[slot, there] = partial(slot, 2 * there + 1 - core).astype(BF16)
            if before_send is not None:
                before_send()
                before_send = None
            to_core(slot, there).start()
        for there in order:
            own[slot, there] = partial(slot, 2 * there + core)

    for load in loads:
        load.wait()
    sides = (page > 0, page < pages - 1)
    for side in (0, 1):
        slot = 2 * side
        partials(slot, wait_barrier if side == 0 else None)
        for there in order:
            to_core(slot, there).wait_recv()

            @pl.when(sides[side])
            def _():
                page_stage[side, there] = (own[slot, there] + from_core[slot, there].astype(F32)).astype(BF16)
                to_page(side, there).start()
    partials(1)
    for there in order:
        to_core(1, there).wait_recv()
        own[1, there] += from_core[1, there].astype(F32)
    for there in order:
        for side in (0, 1):
            @pl.when(sides[1 - side])
            def _():
                to_page(side, there).wait_recv()
                own[1, there] += from_page[side, there].astype(F32)

        if there is not order[-1]:
            chip_stage[there] = own[1, there].astype(BF16)
            to_chip(there).start()
    total = own[1, chip]
    for there in order[:-1]:
        chip_arrived(there)
        total = total + from_chip[there].astype(F32)
    out_ref[...] = total.astype(BF16)
    for there in order:
        for slot in range(3):
            to_core(slot, there).wait_send()
        for side in (0, 1):
            @pl.when(sides[side])
            def _():
                to_page(side, there).wait_send()

        if there is not order[-1]:
            to_chip(there).wait_send()


def on_device(pages, tensors, query, memory, key_weight, value_weight, out_grad, mask_blocks):
    tokens, features = query.shape
    rows, width = memory.shape
    depth = key_weight.shape[0]
    chips = tensors // 2
    anywhere = pl.BlockSpec(memory_space=pl.ANY)
    in_vmem = pl.BlockSpec(memory_space=pltpu.VMEM)
    dma = pltpu.SemaphoreType.DMA
    keys, values = pl.pallas_call(
        functools.partial(project_kernel, pages, tensors),
        out_shape=[jax.ShapeDtypeStruct((3 * rows, features), BF16)] * 2,
        in_specs=[in_vmem, anywhere, anywhere],
        out_specs=[anywhere, anywhere],
        scratch_shapes=[
            pltpu.VMEM((3, tensors, rows, width), BF16),
            pltpu.VMEM((depth, features), BF16),
            pltpu.VMEM((depth, features), BF16),
            pltpu.VMEM((3, rows, features), BF16),
            pltpu.VMEM((3, rows, features), BF16),
            dma((2,)),
            dma((3, 2)),
            dma((6, tensors)),
            dma((3, tensors)),
        ],
        compiler_params=pltpu.CompilerParams(
            collective_id=0, has_side_effects=True, vmem_limit_bytes=VMEM_LIMIT
        ),
        name="gather_project",
    )(memory, key_weight, value_weight)

    heads = 1
    step = heads * HD
    column = lambda i: (0, i)
    attended, query_grad, key_piece, value_piece = pl.pallas_call(
        functools.partial(attend_kernel, pages),
        grid=(features // step,),
        out_shape=[jax.ShapeDtypeStruct((tokens, features), BF16)] * 2
        + [jax.ShapeDtypeStruct((3 * rows, features), BF16)] * 2,
        in_specs=[
            pl.BlockSpec(memory_space=pltpu.SMEM),
            pl.BlockSpec((tokens, step), column),
            pl.BlockSpec((tokens, step), column),
            pl.BlockSpec((3 * rows, step), column),
            pl.BlockSpec((3 * rows, step), column),
        ],
        out_specs=[
            pl.BlockSpec((tokens, step), column),
            pl.BlockSpec((tokens, step), column),
            pl.BlockSpec((3 * rows, step), column),
            pl.BlockSpec((3 * rows, step), column),
        ],
        compiler_params=pltpu.CompilerParams(vmem_limit_bytes=VMEM_LIMIT),
        name="attend",
    )(mask_blocks, query, out_grad, keys, values)

    memory_grad = pl.pallas_call(
        functools.partial(reduce_kernel, pages, tensors),
        out_shape=jax.ShapeDtypeStruct((rows, width), BF16),
        in_specs=[anywhere] * 4,
        out_specs=in_vmem,
        scratch_shapes=[
            pltpu.VMEM((3 * rows, features), BF16),
            pltpu.VMEM((3 * rows, features), BF16),
            pltpu.VMEM((depth, features), BF16),
            pltpu.VMEM((depth, features), BF16),
            pltpu.VMEM((3, chips, rows, width), F32),
            pltpu.VMEM((3, chips, rows, width), BF16),
            pltpu.VMEM((3, chips, rows, width), BF16),
            pltpu.VMEM((2, chips, rows, width), BF16),
            pltpu.VMEM((2, chips, rows, width), BF16),
            pltpu.VMEM((chips, rows, width), BF16),
            pltpu.VMEM((chips, rows, width), BF16),
            dma((4,)),
            dma((3, chips)),
            dma((3, chips)),
            dma((2, chips)),
            dma((2, chips)),
            dma((chips,)),
            dma((chips,)),
        ],
        compiler_params=pltpu.CompilerParams(
            collective_id=1, has_side_effects=True, vmem_limit_bytes=VMEM_LIMIT
        ),
        name="back_project_reduce",
    )(key_piece, value_piece, key_weight, value_weight)
    return attended, query_grad, memory_grad


def solution(mesh):
    placed = (
        P(("groups", "page"), "tensor"),
        P(("groups", "page"), "tensor"),
        P(None, "tensor"),
        P(None, "tensor"),
        P(("groups", "page"), "tensor"),
        P(("groups", "page"), None, None, None),
    )
    return jax.shard_map(
        functools.partial(on_device, mesh.shape["page"], mesh.shape["tensor"]),
        mesh=mesh,
        in_specs=placed,
        out_specs=(
            P(("groups", "page"), "tensor"),
            P(("groups", "page"), "tensor"),
            P(("groups", "page"), "tensor"),
        ),
        check_vma=False,
    )
```

```python
import functools
import math

import jax
import jax.numpy as jnp
from jax import lax
from jax.experimental import pallas as pl
from jax.experimental.pallas import tpu as pltpu
from jax.sharding import PartitionSpec as P

HD = 128
MESH = pl.DeviceIdType.MESH
VMEM_LIMIT = 24 * 1024 * 1024
GATHER_LIMIT = 24 * 1024 * 1024
F32 = jnp.float32
BF16 = jnp.bfloat16


def place():
    page = lax.axis_index("page")
    tensor = lax.axis_index("tensor")
    core = lax.rem(tensor, 2)
    return page, tensor, core, tensor + 1 - 2 * core


def greet(pages, tensors):
    page, tensor, core, sibling = place()
    barrier = pltpu.get_barrier_semaphore()
    chips = tensors // 2

    def signal(where):
        pl.semaphore_signal(barrier, inc=1, device_id=where, device_id_type=MESH)

    signal({"tensor": sibling})
    for d in range(1, chips):
        signal({"tensor": lax.rem(tensor + 2 * d, tensors)})

    @pl.when(page > 0)
    def _():
        signal({"page": page - 1})

    @pl.when(page < pages - 1)
    def _():
        signal({"page": page + 1})

    def wait():
        at_end = jnp.where(page > 0, 1, 0) + jnp.where(page < pages - 1, 1, 0)
        pl.semaphore_wait(barrier, chips + at_end)

    return wait


def remote(src, dst, send, recv, where):
    return pltpu.make_async_remote_copy(
        src_ref=src, dst_ref=dst, send_sem=send, recv_sem=recv, device_id=where, device_id_type=MESH
    )


def project_kernel(
    pages, tensors, mem_ref, wk_hbm, wv_hbm, keys, values,
    gathered, wk, wv, load_sem, send_sem, recv_sem,
):
    page, tensor, core, sibling = place()
    chips = tensors // 2
    rows, width = mem_ref.shape
    features = wk.shape[1]
    tile = min(256, features)

    loads = [
        pltpu.make_async_copy(wk_hbm, wk, load_sem.at[0]),
        pltpu.make_async_copy(wv_hbm, wv, load_sem.at[1]),
    ]
    wait_barrier = greet(pages, tensors)
    for load in loads:
        load.start()
    gathered[1, tensor] = mem_ref[...]
    has_prev = page > 0
    has_next = page < pages - 1

    def to_sibling(src, slot, owner):
        return remote(src, gathered.at[slot, owner], send_sem.at[slot, owner], recv_sem.at[slot, owner], {"tensor": sibling})

    def to_chip(src, d):
        there = lax.rem(tensor + 2 * d, tensors)
        return remote(src, gathered.at[1, tensor], send_sem.at[3, there], recv_sem.at[1, tensor], {"tensor": there})

    def to_next(src, owner):
        return remote(src, gathered.at[0, owner], send_sem.at[4, owner], recv_sem.at[0, owner], {"page": page + 1})

    def to_prev(src, owner):
        return remote(src, gathered.at[2, owner], send_sem.at[5, owner], recv_sem.at[2, owner], {"page": page - 1})

    def arrived(slot, owner):
        remote(
            gathered.at[slot, owner], gathered.at[slot, owner], send_sem.at[0, owner],
            recv_sem.at[slot, owner], {"tensor": sibling},
        ).wait_recv()

    def spread(src, owner):
        @pl.when(has_next)
        def _():
            to_next(src, owner).start()

        @pl.when(has_prev)
        def _():
            to_prev(src, owner).start()

    wait_barrier()
    for d in range(1, chips):
        to_chip(mem_ref, d).start()
    spread(mem_ref, tensor)
    to_sibling(mem_ref, 1, tensor).start()
    peers = [lax.rem(tensor + 2 * d, tensors) for d in range(chips)]
    for owner in peers[1:]:
        arrived(1, owner)
        spread(gathered.at[1, owner], owner)
        to_sibling(gathered.at[1, owner], 1, owner).start()

    def project(slot):
        span = slice(slot * rows, (slot + 1) * rows)

        def step(i, _):
            columns = pl.ds(pl.multiple_of(i * tile, tile), tile)
            whole = jnp.concatenate([gathered[slot, owner] for owner in range(tensors)], axis=1)
            keys[span, columns] = jnp.dot(whole, wk[:, columns], preferred_element_type=F32).astype(BF16)
            values[span, columns] = jnp.dot(whole, wv[:, columns], preferred_element_type=F32).astype(BF16)
            return 0

        lax.fori_loop(0, features // tile, step, 0)

    def other(owner):
        return owner + 1 - 2 * lax.rem(owner, 2)

    def pass_on(k):
        @pl.when(has_prev)
        def _():
            arrived(0, peers[k])
            to_sibling(gathered.at[0, peers[k]], 0, peers[k]).start()

        @pl.when(has_next)
        def _():
            arrived(2, peers[k])
            to_sibling(gathered.at[2, peers[k]], 2, peers[k]).start()

    for owner in peers:
        arrived(1, other(owner))
    for load in loads:
        load.wait()
    project(1)
    for k in range(chips):
        pass_on(k)
    for slot, there in ((0, has_prev), (2, has_next)):
        @pl.when(there)
        def _():
            for owner in peers:
                arrived(slot, other(owner))
            project(slot)

        @pl.when(jnp.logical_not(there))
        def _():
            span = slice(slot * rows, (slot + 1) * rows)
            keys[span] = jnp.zeros((rows, features), BF16)
            values[span] = jnp.zeros((rows, features), BF16)

    for d in range(1, chips):
        to_chip(mem_ref, d).wait_send()
    for owner in peers:
        to_sibling(mem_ref, 1, owner).wait_send()

        @pl.when(has_next)
        def _():
            to_next(mem_ref, owner).wait_send()
            to_sibling(mem_ref, 2, owner).wait_send()

        @pl.when(has_prev)
        def _():
            to_prev(mem_ref, owner).wait_send()
            to_sibling(mem_ref, 0, owner).wait_send()


def attend_kernel(pages, mask_ref, q_ref, g_ref, k_ref, v_ref, att_ref, qg_ref, kp_ref, vp_ref):
    page = lax.axis_index("page")
    slots, memory_blocks, query_blocks = mask_ref.shape[1:]
    block = q_ref.shape[0] // query_blocks
    scale = 1.0 / math.sqrt(HD)
    rate = scale * math.log2(math.e)
    nt = (((1,), (1,)), ((), ()))
    tn = (((0,), (0,)), ((), ()))
    heads = q_ref.shape[1] // HD
    bias = {}
    for slot in range(slots):
        source = page + (slot - 1)
        live = jnp.logical_and(source >= 0, source < pages)
        for tb in range(query_blocks):
            for mb in range(memory_blocks):
                seen = jnp.logical_and(mask_ref[0, slot, mb, tb] > 0, live)
                bias[tb, slot * memory_blocks + mb] = jnp.where(seen, 0.0, -1e30).astype(F32)

    def columns(head):
        return slice(head * HD, (head + 1) * HD)

    def products(head):
        cols = columns(head)
        return (
            lax.dot_general(k_ref[:, cols], q_ref[:, cols], nt, preferred_element_type=F32),
            lax.dot_general(v_ref[:, cols], g_ref[:, cols], nt, preferred_element_type=F32),
        )

    def softmax(scores, weight_grad):
        rounded, score_grads = [], []
        for tb in range(query_blocks):
            span = slice(tb * block, (tb + 1) * block)
            biased = jnp.concatenate(
                [
                    scores[i * block : (i + 1) * block, span] + bias[tb, i]
                    for i in range(slots * memory_blocks)
                ],
                axis=0,
            )
            top = jnp.max(biased, axis=0, keepdims=True)
            exponent = jnp.exp2((biased - top) * rate)
            weights = exponent * (1.0 / jnp.sum(exponent, axis=0, keepdims=True))
            rounded.append(weights.astype(BF16))
            grad = weight_grad[:, span]
            inner = jnp.sum(weights * grad, axis=0, keepdims=True)
            score_grads.append((weights * (grad - inner)).astype(BF16))
        return jnp.concatenate(rounded, axis=1), jnp.concatenate(score_grads, axis=1)

    def outputs(head, rounded, score_grad):
        cols = columns(head)
        att = lax.dot_general(v_ref[:, cols], rounded, tn, preferred_element_type=F32)
        att_ref[:, cols] = att.T.astype(BF16)
        qg = lax.dot_general(k_ref[:, cols], score_grad, tn, preferred_element_type=F32) * scale
        qg_ref[:, cols] = qg.T.astype(BF16)
        vp_ref[:, cols] = jnp.dot(rounded, g_ref[:, cols], preferred_element_type=F32).astype(BF16)
        kp = jnp.dot(score_grad, q_ref[:, cols], preferred_element_type=F32) * scale
        kp_ref[:, cols] = kp.astype(BF16)

    ahead, ready = products(0), None
    for head in range(heads):
        now = ahead
        if head + 1 < heads:
            ahead = products(head + 1)
        done = softmax(*now)
        if ready is not None:
            outputs(head - 1, *ready)
        ready = done
    outputs(heads - 1, *ready)


def reduce_kernel(
    pages, tensors, kp, vp, wk, wv, out_ref,
    own, stage, from_core, page_stage, from_page, chip_stage, from_chip,
    core_send, core_recv, page_send, page_recv, chip_send, chip_recv,
):
    page, tensor, core, sibling = place()
    chips = tensors // 2
    chip = tensor // 2
    rows, width = out_ref.shape
    nt = (((1,), (1,)), ((), ()))
    wait_barrier = greet(pages, tensors)
    def partial(slot, group):
        take = pl.ds(pl.multiple_of(group * width, width), width)
        span = slice(slot * rows, (slot + 1) * rows)
        return lax.dot_general(kp[span], wk[take], nt, preferred_element_type=F32) + lax.dot_general(
            vp[span], wv[take], nt, preferred_element_type=F32
        )

    def to_core(slot, there):
        return remote(
            stage.at[slot, there], from_core.at[slot, there], core_send.at[slot, there],
            core_recv.at[slot, there], {"tensor": sibling},
        )

    def to_page(side, there):
        return remote(
            page_stage.at[side, there], from_page.at[side, there], page_send.at[side, there],
            page_recv.at[side, there], {"page": page - 1 + 2 * side},
        )

    def to_chip(there):
        return remote(
            chip_stage.at[there], from_chip.at[chip], chip_send.at[there], chip_recv.at[chip],
            {"tensor": 2 * there + core},
        )

    def chip_arrived(there):
        remote(
            chip_stage.at[there], from_chip.at[there], chip_send.at[there], chip_recv.at[there],
            {"tensor": 2 * there + core},
        ).wait_recv()

    order = [lax.rem(chip + 1 + k, chips) for k in range(chips)]

    def for_core(slot, there):
        stage[slot, there] = partial(slot, 2 * there + 1 - core).astype(BF16)

    sides = (page > 0, page < pages - 1)
    for there in order:
        for slot in (0, 2):
            for_core(slot, there)
            if there is order[0] and slot == 0:
                wait_barrier()
            to_core(slot, there).start()
        for slot in (0, 2):
            own[slot, there] = partial(slot, 2 * there + core)
            to_core(slot, there).wait_recv()

            @pl.when(sides[slot // 2])
            def _():
                page_stage[slot // 2, there] = (own[slot, there] + from_core[slot, there].astype(F32)).astype(BF16)
                to_page(slot // 2, there).start()
    for there in order:
        for_core(1, there)
        to_core(1, there).start()
    for there in order:
        own[1, there] = partial(1, 2 * there + core)
    for there in order:
        to_core(1, there).wait_recv()
        own[1, there] += from_core[1, there].astype(F32)
    for there in order:
        for side in (0, 1):
            @pl.when(sides[1 - side])
            def _():
                to_page(side, there).wait_recv()
                own[1, there] += from_page[side, there].astype(F32)

        if there is not order[-1]:
            chip_stage[there] = own[1, there].astype(BF16)
            to_chip(there).start()
    total = own[1, chip]
    for there in order[:-1]:
        chip_arrived(there)
        total = total + from_chip[there].astype(F32)
    out_ref[...] = total.astype(BF16)
    for there in order:
        for slot in range(3):
            to_core(slot, there).wait_send()
        for side in (0, 1):
            @pl.when(sides[side])
            def _():
                to_page(side, there).wait_send()

        if there is not order[-1]:
            to_chip(there).wait_send()


def on_device(pages, tensors, query, memory, key_weight, value_weight, out_grad, mask_blocks):
    tokens, features = query.shape
    rows, width = memory.shape
    depth = key_weight.shape[0]
    chips = tensors // 2
    in_vmem = pl.BlockSpec(memory_space=pltpu.VMEM)
    in_hbm = pl.BlockSpec(memory_space=pltpu.HBM)
    dma = pltpu.SemaphoreType.DMA
    keys, values = pl.pallas_call(
        functools.partial(project_kernel, pages, tensors),
        out_shape=[jax.ShapeDtypeStruct((3 * rows, features), BF16)] * 2,
        in_specs=[in_vmem, in_hbm, in_hbm],
        out_specs=[in_vmem, in_vmem],
        scratch_shapes=[
            pltpu.VMEM((3, tensors, rows, width), BF16),
            pltpu.VMEM((depth, features), BF16),
            pltpu.VMEM((depth, features), BF16),
            dma((2,)),
            dma((6, tensors)),
            dma((3, tensors)),
        ],
        compiler_params=pltpu.CompilerParams(
            collective_id=0, has_side_effects=True, vmem_limit_bytes=GATHER_LIMIT
        ),
        name="gather_project",
    )(memory, *[pltpu.with_memory_space_constraint(w, pltpu.HBM) for w in (key_weight, value_weight)])

    heads = 2
    step = heads * HD
    column = lambda i: (0, i)
    attended, query_grad, key_piece, value_piece = pl.pallas_call(
        functools.partial(attend_kernel, pages),
        grid=(features // step,),
        out_shape=[jax.ShapeDtypeStruct((tokens, features), BF16)] * 2
        + [jax.ShapeDtypeStruct((3 * rows, features), BF16)] * 2,
        in_specs=[
            pl.BlockSpec(memory_space=pltpu.SMEM),
            pl.BlockSpec((tokens, step), column),
            pl.BlockSpec((tokens, step), column),
            pl.BlockSpec((3 * rows, step), column),
            pl.BlockSpec((3 * rows, step), column),
        ],
        out_specs=[
            pl.BlockSpec((tokens, step), column),
            pl.BlockSpec((tokens, step), column),
            pl.BlockSpec((3 * rows, step), column),
            pl.BlockSpec((3 * rows, step), column),
        ],
        compiler_params=pltpu.CompilerParams(vmem_limit_bytes=VMEM_LIMIT),
        name="attend",
    )(jnp.swapaxes(mask_blocks, 2, 3), query, out_grad, keys, values)

    memory_grad = pl.pallas_call(
        functools.partial(reduce_kernel, pages, tensors),
        out_shape=jax.ShapeDtypeStruct((rows, width), BF16),
        in_specs=[in_vmem] * 4,
        out_specs=in_vmem,
        scratch_shapes=[
            pltpu.VMEM((3, chips, rows, width), F32),
            pltpu.VMEM((3, chips, rows, width), BF16),
            pltpu.VMEM((3, chips, rows, width), BF16),
            pltpu.VMEM((2, chips, rows, width), BF16),
            pltpu.VMEM((2, chips, rows, width), BF16),
            pltpu.VMEM((chips, rows, width), BF16),
            pltpu.VMEM((chips, rows, width), BF16),
            dma((3, chips)),
            dma((3, chips)),
            dma((2, chips)),
            dma((2, chips)),
            dma((chips,)),
            dma((chips,)),
        ],
        compiler_params=pltpu.CompilerParams(
            collective_id=1, has_side_effects=True, vmem_limit_bytes=VMEM_LIMIT
        ),
        name="back_project_reduce",
    )(key_piece, value_piece, key_weight, value_weight)
    return attended, query_grad, memory_grad


def solution(mesh):
    placed = (
        P(("groups", "page"), "tensor"),
        P(("groups", "page"), "tensor"),
        P(None, "tensor"),
        P(None, "tensor"),
        P(("groups", "page"), "tensor"),
        P(("groups", "page"), None, None, None),
    )
    return jax.shard_map(
        functools.partial(on_device, mesh.shape["page"], mesh.shape["tensor"]),
        mesh=mesh,
        in_specs=placed,
        out_specs=(
            P(("groups", "page"), "tensor"),
            P(("groups", "page"), "tensor"),
            P(("groups", "page"), "tensor"),
        ),
        check_vma=False,
    )
```

```python
import functools
import math

import jax
import jax.numpy as jnp
from jax import lax
from jax.experimental import pallas as pl
from jax.experimental.pallas import tpu as pltpu
from jax.sharding import PartitionSpec as P

HD = 128
MESH = pl.DeviceIdType.MESH
VMEM_LIMIT = 24 * 1024 * 1024
GATHER_LIMIT = 24 * 1024 * 1024
F32 = jnp.float32
BF16 = jnp.bfloat16


def place():
    page = lax.axis_index("page")
    tensor = lax.axis_index("tensor")
    core = lax.rem(tensor, 2)
    return page, tensor, core, tensor + 1 - 2 * core


def greet(pages, tensors):
    page, tensor, core, sibling = place()
    barrier = pltpu.get_barrier_semaphore()
    chips = tensors // 2

    def signal(where):
        pl.semaphore_signal(barrier, inc=1, device_id=where, device_id_type=MESH)

    signal({"tensor": sibling})
    for d in range(1, chips):
        signal({"tensor": lax.rem(tensor + 2 * d, tensors)})

    @pl.when(page > 0)
    def _():
        signal({"page": page - 1})

    @pl.when(page < pages - 1)
    def _():
        signal({"page": page + 1})

    def wait():
        at_end = jnp.where(page > 0, 1, 0) + jnp.where(page < pages - 1, 1, 0)
        pl.semaphore_wait(barrier, chips + at_end)

    return wait


def remote(src, dst, send, recv, where):
    return pltpu.make_async_remote_copy(
        src_ref=src, dst_ref=dst, send_sem=send, recv_sem=recv, device_id=where, device_id_type=MESH
    )


def project_kernel(
    pages, tensors, mem_ref, wk_hbm, wv_hbm, keys, values,
    gathered, wk, wv, load_sem, send_sem, recv_sem,
):
    page, tensor, core, sibling = place()
    chips = tensors // 2
    rows, width = mem_ref.shape
    features = wk.shape[1]
    tile = min(256, features)

    loads = [
        pltpu.make_async_copy(mem_ref, gathered.at[1, tensor], load_sem.at[2]),
        pltpu.make_async_copy(wk_hbm, wk, load_sem.at[0]),
        pltpu.make_async_copy(wv_hbm, wv, load_sem.at[1]),
    ]
    wait_barrier = greet(pages, tensors)
    for load in loads:
        load.start()
    has_prev = page > 0
    has_next = page < pages - 1

    def to_sibling(src, slot, owner):
        return remote(src, gathered.at[slot, owner], send_sem.at[slot, owner], recv_sem.at[slot, owner], {"tensor": sibling})

    def to_chip(src, d):
        there = lax.rem(tensor + 2 * d, tensors)
        return remote(src, gathered.at[1, tensor], send_sem.at[3, there], recv_sem.at[1, tensor], {"tensor": there})

    def to_next(src, owner):
        return remote(src, gathered.at[0, owner], send_sem.at[4, owner], recv_sem.at[0, owner], {"page": page + 1})

    def to_prev(src, owner):
        return remote(src, gathered.at[2, owner], send_sem.at[5, owner], recv_sem.at[2, owner], {"page": page - 1})

    def arrived(slot, owner):
        remote(
            gathered.at[slot, owner], gathered.at[slot, owner], send_sem.at[0, owner],
            recv_sem.at[slot, owner], {"tensor": sibling},
        ).wait_recv()

    def spread(src, owner):
        @pl.when(has_next)
        def _():
            to_next(src, owner).start()

        @pl.when(has_prev)
        def _():
            to_prev(src, owner).start()

    wait_barrier()
    for d in range(1, chips):
        to_chip(mem_ref, d).start()
    spread(mem_ref, tensor)
    to_sibling(mem_ref, 1, tensor).start()
    peers = [lax.rem(tensor + 2 * d, tensors) for d in range(chips)]
    for owner in peers[1:]:
        arrived(1, owner)
        spread(gathered.at[1, owner], owner)
        to_sibling(gathered.at[1, owner], 1, owner).start()

    def project(slot):
        span = slice(slot * rows, (slot + 1) * rows)

        def step(i, _):
            columns = pl.ds(pl.multiple_of(i * tile, tile), tile)
            whole = jnp.concatenate([gathered[slot, owner] for owner in range(tensors)], axis=1)
            keys[span, columns] = jnp.dot(whole, wk[:, columns], preferred_element_type=F32).astype(BF16)
            values[span, columns] = jnp.dot(whole, wv[:, columns], preferred_element_type=F32).astype(BF16)
            return 0

        lax.fori_loop(0, features // tile, step, 0)

    def other(owner):
        return owner + 1 - 2 * lax.rem(owner, 2)

    def pass_on(k):
        @pl.when(has_prev)
        def _():
            arrived(0, peers[k])
            to_sibling(gathered.at[0, peers[k]], 0, peers[k]).start()

        @pl.when(has_next)
        def _():
            arrived(2, peers[k])
            to_sibling(gathered.at[2, peers[k]], 2, peers[k]).start()

    for owner in peers:
        arrived(1, other(owner))
    for load in loads:
        load.wait()
    project(1)
    for k in range(chips):
        pass_on(k)
    for slot, there in ((0, has_prev), (2, has_next)):
        @pl.when(there)
        def _():
            for owner in peers:
                arrived(slot, other(owner))
            project(slot)

        @pl.when(jnp.logical_not(there))
        def _():
            span = slice(slot * rows, (slot + 1) * rows)
            keys[span] = jnp.zeros((rows, features), BF16)
            values[span] = jnp.zeros((rows, features), BF16)

    for d in range(1, chips):
        to_chip(mem_ref, d).wait_send()
    for owner in peers:
        to_sibling(mem_ref, 1, owner).wait_send()

        @pl.when(has_next)
        def _():
            to_next(mem_ref, owner).wait_send()
            to_sibling(mem_ref, 2, owner).wait_send()

        @pl.when(has_prev)
        def _():
            to_prev(mem_ref, owner).wait_send()
            to_sibling(mem_ref, 0, owner).wait_send()


def attend_kernel(pages, mask_ref, q_ref, g_ref, k_ref, v_ref, att_ref, qg_ref, kp_ref, vp_ref):
    page = lax.axis_index("page")
    slots, memory_blocks, query_blocks = mask_ref.shape[1:]
    block = q_ref.shape[0] // query_blocks
    scale = 1.0 / math.sqrt(HD)
    rate = scale * math.log2(math.e)
    nt = (((1,), (1,)), ((), ()))
    tn = (((0,), (0,)), ((), ()))
    heads = q_ref.shape[1] // HD
    bias = {}
    for slot in range(slots):
        source = page + (slot - 1)
        live = jnp.logical_and(source >= 0, source < pages)
        for tb in range(query_blocks):
            for mb in range(memory_blocks):
                seen = jnp.logical_and(mask_ref[0, slot, mb, tb] > 0, live)
                bias[tb, slot * memory_blocks + mb] = jnp.where(seen, 0.0, -1e30).astype(F32)

    def columns(head):
        return slice(head * HD, (head + 1) * HD)

    def products(head):
        cols = columns(head)
        return (
            lax.dot_general(k_ref[:, cols], q_ref[:, cols], nt, preferred_element_type=F32),
            lax.dot_general(v_ref[:, cols], g_ref[:, cols], nt, preferred_element_type=F32),
        )

    def softmax(scores, weight_grad):
        rounded, score_grads = [], []
        for tb in range(query_blocks):
            span = slice(tb * block, (tb + 1) * block)
            biased = jnp.concatenate(
                [
                    scores[i * block : (i + 1) * block, span] + bias[tb, i]
                    for i in range(slots * memory_blocks)
                ],
                axis=0,
            )
            top = jnp.max(biased, axis=0, keepdims=True)
            exponent = jnp.exp2((biased - top) * rate)
            weights = exponent * (1.0 / jnp.sum(exponent, axis=0, keepdims=True))
            rounded.append(weights.astype(BF16))
            grad = weight_grad[:, span]
            inner = jnp.sum(weights * grad, axis=0, keepdims=True)
            score_grads.append((weights * (grad - inner)).astype(BF16))
        return jnp.concatenate(rounded, axis=1), jnp.concatenate(score_grads, axis=1)

    def outputs(head, rounded, score_grad):
        cols = columns(head)
        att = lax.dot_general(v_ref[:, cols], rounded, tn, preferred_element_type=F32)
        att_ref[:, cols] = att.T.astype(BF16)
        qg = lax.dot_general(k_ref[:, cols], score_grad, tn, preferred_element_type=F32) * scale
        qg_ref[:, cols] = qg.T.astype(BF16)
        vp_ref[:, cols] = jnp.dot(rounded, g_ref[:, cols], preferred_element_type=F32).astype(BF16)
        kp = jnp.dot(score_grad, q_ref[:, cols], preferred_element_type=F32) * scale
        kp_ref[:, cols] = kp.astype(BF16)

    ahead, ready = products(0), None
    for head in range(heads):
        now = ahead
        if head + 1 < heads:
            ahead = products(head + 1)
        done = softmax(*now)
        if ready is not None:
            outputs(head - 1, *ready)
        ready = done
    outputs(heads - 1, *ready)


def reduce_kernel(
    pages, tensors, kp, vp, wk, wv, out_ref,
    own, stage, from_core, page_stage, from_page, chip_stage, from_chip,
    core_send, core_recv, page_send, page_recv, chip_send, chip_recv,
):
    page, tensor, core, sibling = place()
    chips = tensors // 2
    chip = tensor // 2
    rows, width = out_ref.shape
    nt = (((1,), (1,)), ((), ()))
    wait_barrier = greet(pages, tensors)
    def partial(slots, group):
        take = pl.ds(pl.multiple_of(group * width, width), width)

        def rows_of(piece):
            return jnp.concatenate([piece[slot * rows : (slot + 1) * rows] for slot in slots], axis=0)

        product = lax.dot_general(rows_of(kp), wk[take], nt, preferred_element_type=F32) + lax.dot_general(
            rows_of(vp), wv[take], nt, preferred_element_type=F32
        )
        return [product[i * rows : (i + 1) * rows] for i in range(len(slots))]

    def to_core(slot, there):
        return remote(
            stage.at[slot, there], from_core.at[slot, there], core_send.at[slot, there],
            core_recv.at[slot, there], {"tensor": sibling},
        )

    def to_page(side, there):
        return remote(
            page_stage.at[side, there], from_page.at[side, there], page_send.at[side, there],
            page_recv.at[side, there], {"page": page - 1 + 2 * side},
        )

    def to_chip(there):
        return remote(
            chip_stage.at[there], from_chip.at[chip], chip_send.at[there], chip_recv.at[chip],
            {"tensor": 2 * there + core},
        )

    def chip_arrived(there):
        remote(
            chip_stage.at[there], from_chip.at[there], chip_send.at[there], chip_recv.at[there],
            {"tensor": 2 * there + core},
        ).wait_recv()

    order = [lax.rem(chip + 1 + k, chips) for k in range(chips)]

    sides = (page > 0, page < pages - 1)

    def for_core(slots, there):
        for slot, product in zip(slots, partial(slots, 2 * there + 1 - core)):
            stage[slot, there] = product.astype(BF16)

    for there in order:
        for_core((0, 2), there)
        if there is order[0]:
            wait_barrier()
        for slot in (0, 2):
            to_core(slot, there).start()
        mine = partial((0, 2), 2 * there + core)
        for slot, product in zip((0, 2), mine):
            own[slot, there] = product
        for slot in (0, 2):
            to_core(slot, there).wait_recv()

            @pl.when(sides[slot // 2])
            def _():
                page_stage[slot // 2, there] = (own[slot, there] + from_core[slot, there].astype(F32)).astype(BF16)
                to_page(slot // 2, there).start()
    for there in order:
        for_core((1,), there)
        to_core(1, there).start()
    for there in order:
        own[1, there] = partial((1,), 2 * there + core)[0]
    for there in order:
        to_core(1, there).wait_recv()
        own[1, there] += from_core[1, there].astype(F32)
    for there in order:
        for side in (0, 1):
            @pl.when(sides[1 - side])
            def _():
                to_page(side, there).wait_recv()
                own[1, there] += from_page[side, there].astype(F32)

        if there is not order[-1]:
            chip_stage[there] = own[1, there].astype(BF16)
            to_chip(there).start()
    total = own[1, chip]
    for there in order[:-1]:
        chip_arrived(there)
        total = total + from_chip[there].astype(F32)
    out_ref[...] = total.astype(BF16)
    for there in order:
        for slot in range(3):
            to_core(slot, there).wait_send()
        for side in (0, 1):
            @pl.when(sides[side])
            def _():
                to_page(side, there).wait_send()

        if there is not order[-1]:
            to_chip(there).wait_send()


def on_device(pages, tensors, query, memory, key_weight, value_weight, out_grad, mask_blocks):
    tokens, features = query.shape
    rows, width = memory.shape
    depth = key_weight.shape[0]
    chips = tensors // 2
    in_vmem = pl.BlockSpec(memory_space=pltpu.VMEM)
    in_hbm = pl.BlockSpec(memory_space=pltpu.HBM)
    dma = pltpu.SemaphoreType.DMA
    keys, values = pl.pallas_call(
        functools.partial(project_kernel, pages, tensors),
        out_shape=[jax.ShapeDtypeStruct((3 * rows, features), BF16)] * 2,
        in_specs=[in_hbm] * 3,
        out_specs=[in_vmem, in_vmem],
        scratch_shapes=[
            pltpu.VMEM((3, tensors, rows, width), BF16),
            pltpu.VMEM((depth, features), BF16),
            pltpu.VMEM((depth, features), BF16),
            dma((3,)),
            dma((6, tensors)),
            dma((3, tensors)),
        ],
        compiler_params=pltpu.CompilerParams(
            collective_id=0, has_side_effects=True, vmem_limit_bytes=GATHER_LIMIT
        ),
        name="gather_project",
    )(*[pltpu.with_memory_space_constraint(a, pltpu.HBM) for a in (memory, key_weight, value_weight)])

    heads = 2
    step = heads * HD
    column = lambda i: (0, i)
    attended, query_grad, key_piece, value_piece = pl.pallas_call(
        functools.partial(attend_kernel, pages),
        grid=(features // step,),
        out_shape=[jax.ShapeDtypeStruct((tokens, features), BF16)] * 2
        + [jax.ShapeDtypeStruct((3 * rows, features), BF16)] * 2,
        in_specs=[
            pl.BlockSpec(memory_space=pltpu.SMEM),
            pl.BlockSpec((tokens, step), column),
            pl.BlockSpec((tokens, step), column),
            pl.BlockSpec((3 * rows, step), column),
            pl.BlockSpec((3 * rows, step), column),
        ],
        out_specs=[
            pl.BlockSpec((tokens, step), column),
            pl.BlockSpec((tokens, step), column),
            pl.BlockSpec((3 * rows, step), column),
            pl.BlockSpec((3 * rows, step), column),
        ],
        compiler_params=pltpu.CompilerParams(vmem_limit_bytes=VMEM_LIMIT),
        name="attend",
    )(jnp.swapaxes(mask_blocks, 2, 3), query, out_grad, keys, values)

    memory_grad = pl.pallas_call(
        functools.partial(reduce_kernel, pages, tensors),
        out_shape=jax.ShapeDtypeStruct((rows, width), BF16),
        in_specs=[in_vmem] * 4,
        out_specs=in_vmem,
        scratch_shapes=[
            pltpu.VMEM((3, chips, rows, width), F32),
            pltpu.VMEM((3, chips, rows, width), BF16),
            pltpu.VMEM((3, chips, rows, width), BF16),
            pltpu.VMEM((2, chips, rows, width), BF16),
            pltpu.VMEM((2, chips, rows, width), BF16),
            pltpu.VMEM((chips, rows, width), BF16),
            pltpu.VMEM((chips, rows, width), BF16),
            dma((3, chips)),
            dma((3, chips)),
            dma((2, chips)),
            dma((2, chips)),
            dma((chips,)),
            dma((chips,)),
        ],
        compiler_params=pltpu.CompilerParams(
            collective_id=1, has_side_effects=True, vmem_limit_bytes=VMEM_LIMIT
        ),
        name="back_project_reduce",
    )(key_piece, value_piece, key_weight, value_weight)
    return attended, query_grad, memory_grad


def solution(mesh):
    placed = (
        P(("groups", "page"), "tensor"),
        P(("groups", "page"), "tensor"),
        P(None, "tensor"),
        P(None, "tensor"),
        P(("groups", "page"), "tensor"),
        P(("groups", "page"), None, None, None),
    )
    return jax.shard_map(
        functools.partial(on_device, mesh.shape["page"], mesh.shape["tensor"]),
        mesh=mesh,
        in_specs=placed,
        out_specs=(
            P(("groups", "page"), "tensor"),
            P(("groups", "page"), "tensor"),
            P(("groups", "page"), "tensor"),
        ),
        check_vma=False,
    )
```

```python
import functools
import math

import jax
import jax.numpy as jnp
from jax import lax
from jax.experimental import pallas as pl
from jax.experimental.pallas import tpu as pltpu
from jax.sharding import PartitionSpec as P

HD = 128
HALVES = 2
MESH = pl.DeviceIdType.MESH
VMEM_LIMIT = 24 * 1024 * 1024
GATHER_LIMIT = 24 * 1024 * 1024
F32 = jnp.float32
BF16 = jnp.bfloat16


def place():
    page = lax.axis_index("page")
    tensor = lax.axis_index("tensor")
    core = lax.rem(tensor, 2)
    return page, tensor, core, tensor + 1 - 2 * core


def greet(pages, tensors):
    page, tensor, core, sibling = place()
    barrier = pltpu.get_barrier_semaphore()
    chips = tensors // 2

    def signal(where):
        pl.semaphore_signal(barrier, inc=1, device_id=where, device_id_type=MESH)

    signal({"tensor": sibling})
    for d in range(1, chips):
        signal({"tensor": lax.rem(tensor + 2 * d, tensors)})

    @pl.when(page > 0)
    def _():
        signal({"page": page - 1})

    @pl.when(page < pages - 1)
    def _():
        signal({"page": page + 1})

    def wait():
        at_end = jnp.where(page > 0, 1, 0) + jnp.where(page < pages - 1, 1, 0)
        pl.semaphore_wait(barrier, chips + at_end)

    return wait


def remote(src, dst, send, recv, where):
    return pltpu.make_async_remote_copy(
        src_ref=src, dst_ref=dst, send_sem=send, recv_sem=recv, device_id=where, device_id_type=MESH
    )


def project_kernel(
    pages, tensors, mem_ref, wk_hbm, wv_hbm, keys, values,
    gathered, wk, wv, load_sem, send_sem, recv_sem,
):
    page, tensor, core, sibling = place()
    chips = tensors // 2
    rows, width = mem_ref.shape
    features = wk.shape[1]
    tile = min(256, features)

    loads = [
        pltpu.make_async_copy(mem_ref, gathered.at[1, tensor], load_sem.at[2]),
        pltpu.make_async_copy(wk_hbm, wk, load_sem.at[0]),
        pltpu.make_async_copy(wv_hbm, wv, load_sem.at[1]),
    ]
    wait_barrier = greet(pages, tensors)
    for load in loads:
        load.start()
    has_prev = page > 0
    has_next = page < pages - 1

    half = rows // HALVES

    def part(ref, h):
        return ref.at[pl.ds(h * half, half)]

    def shard(slot, owner, h):
        return gathered.at[slot, owner, pl.ds(h * half, half)]

    def to_sibling(src, slot, owner, h):
        return remote(src, shard(slot, owner, h), send_sem.at[slot, owner, h], recv_sem.at[slot, owner, h], {"tensor": sibling})

    def to_chip(d, h):
        there = lax.rem(tensor + 2 * d, tensors)
        return remote(part(mem_ref, h), shard(1, tensor, h), send_sem.at[3, there, h], recv_sem.at[1, tensor, h], {"tensor": there})

    def to_next(src, owner, h):
        return remote(src, shard(0, owner, h), send_sem.at[4, owner, h], recv_sem.at[0, owner, h], {"page": page + 1})

    def to_prev(src, owner, h):
        return remote(src, shard(2, owner, h), send_sem.at[5, owner, h], recv_sem.at[2, owner, h], {"page": page - 1})

    def arrived(slot, owner, h):
        here = shard(slot, owner, h)
        remote(here, here, send_sem.at[0, owner, h], recv_sem.at[slot, owner, h], {"tensor": sibling}).wait_recv()

    def spread(src, owner, h):
        @pl.when(has_next)
        def _():
            to_next(src, owner, h).start()

        @pl.when(has_prev)
        def _():
            to_prev(src, owner, h).start()

    wait_barrier()
    for h in range(HALVES):
        for d in range(1, chips):
            to_chip(d, h).start()
        spread(part(mem_ref, h), tensor, h)
    for h in range(HALVES):
        to_sibling(part(mem_ref, h), 1, tensor, h).start()
    peers = [lax.rem(tensor + 2 * d, tensors) for d in range(chips)]
    for owner in peers[1:]:
        for h in range(HALVES):
            arrived(1, owner, h)
            spread(shard(1, owner, h), owner, h)
            to_sibling(shard(1, owner, h), 1, owner, h).start()

    def project(slots):
        def step(i, _):
            columns = pl.ds(pl.multiple_of(i * tile, tile), tile)
            whole = jnp.concatenate(
                [
                    jnp.concatenate([gathered[slot, owner] for owner in range(tensors)], axis=1)
                    for slot in slots
                ],
                axis=0,
            )
            for weight, out in ((wk, keys), (wv, values)):
                product = jnp.dot(whole, weight[:, columns], preferred_element_type=F32).astype(BF16)
                for j, slot in enumerate(slots):
                    out[slot * rows : (slot + 1) * rows, columns] = product[j * rows : (j + 1) * rows]
            return 0

        lax.fori_loop(0, features // tile, step, 0)

    def other(owner):
        return owner + 1 - 2 * lax.rem(owner, 2)

    def pass_on(owner, h):
        for slot, there in ((0, has_prev), (2, has_next)):
            @pl.when(there)
            def _():
                arrived(slot, owner, h)
                to_sibling(shard(slot, owner, h), slot, owner, h).start()

    for owner in peers:
        for h in range(HALVES):
            arrived(1, other(owner), h)
    for load in loads:
        load.wait()
    project((1,))
    for owner in peers:
        for h in range(HALVES):
            pass_on(owner, h)
    for slot, there in ((0, has_prev), (2, has_next)):
        @pl.when(there)
        def _():
            for owner in peers:
                for h in range(HALVES):
                    arrived(slot, other(owner), h)

        @pl.when(jnp.logical_not(there))
        def _():
            gathered[slot] = jnp.zeros(gathered.shape[1:], BF16)

    project((0, 2))
    for h in range(HALVES):
        for d in range(1, chips):
            to_chip(d, h).wait_send()
        for owner in peers:
            src = part(mem_ref, h)
            to_sibling(src, 1, owner, h).wait_send()

            @pl.when(has_next)
            def _():
                to_next(src, owner, h).wait_send()
                to_sibling(src, 2, owner, h).wait_send()

            @pl.when(has_prev)
            def _():
                to_prev(src, owner, h).wait_send()
                to_sibling(src, 0, owner, h).wait_send()


def attend_kernel(pages, mask_ref, q_ref, g_ref, k_ref, v_ref, att_ref, qg_ref, kp_ref, vp_ref):
    page = lax.axis_index("page")
    slots, memory_blocks, query_blocks = mask_ref.shape[1:]
    block = q_ref.shape[0] // query_blocks
    scale = 1.0 / math.sqrt(HD)
    rate = scale * math.log2(math.e)
    nt = (((1,), (1,)), ((), ()))
    tn = (((0,), (0,)), ((), ()))
    heads = q_ref.shape[1] // HD
    bias = {}
    for slot in range(slots):
        source = page + (slot - 1)
        live = jnp.logical_and(source >= 0, source < pages)
        for tb in range(query_blocks):
            for mb in range(memory_blocks):
                seen = jnp.logical_and(mask_ref[0, slot, mb, tb] > 0, live)
                bias[tb, slot * memory_blocks + mb] = jnp.where(seen, 0.0, -1e30).astype(F32)

    def columns(head):
        return slice(head * HD, (head + 1) * HD)

    def products(head):
        cols = columns(head)
        return (
            lax.dot_general(k_ref[:, cols], q_ref[:, cols], nt, preferred_element_type=F32),
            lax.dot_general(v_ref[:, cols], g_ref[:, cols], nt, preferred_element_type=F32),
        )

    def softmax(scores, weight_grad):
        rounded, score_grads = [], []
        for tb in range(query_blocks):
            span = slice(tb * block, (tb + 1) * block)
            biased = jnp.concatenate(
                [
                    scores[i * block : (i + 1) * block, span] + bias[tb, i]
                    for i in range(slots * memory_blocks)
                ],
                axis=0,
            )
            top = jnp.max(biased, axis=0, keepdims=True)
            exponent = jnp.exp2((biased - top) * rate)
            weights = exponent * (1.0 / jnp.sum(exponent, axis=0, keepdims=True))
            rounded.append(weights.astype(BF16))
            grad = weight_grad[:, span]
            inner = jnp.sum(weights * grad, axis=0, keepdims=True)
            score_grads.append((weights * (grad - inner)).astype(BF16))
        return jnp.concatenate(rounded, axis=1), jnp.concatenate(score_grads, axis=1)

    def outputs(head, rounded, score_grad):
        cols = columns(head)
        att = lax.dot_general(v_ref[:, cols], rounded, tn, preferred_element_type=F32)
        att_ref[:, cols] = att.T.astype(BF16)
        qg = lax.dot_general(k_ref[:, cols], score_grad, tn, preferred_element_type=F32) * scale
        qg_ref[:, cols] = qg.T.astype(BF16)
        vp_ref[:, cols] = jnp.dot(rounded, g_ref[:, cols], preferred_element_type=F32).astype(BF16)
        kp = jnp.dot(score_grad, q_ref[:, cols], preferred_element_type=F32) * scale
        kp_ref[:, cols] = kp.astype(BF16)

    ahead, ready = products(0), None
    for head in range(heads):
        now = ahead
        if head + 1 < heads:
            ahead = products(head + 1)
        done = softmax(*now)
        if ready is not None:
            outputs(head - 1, *ready)
        ready = done
    outputs(heads - 1, *ready)


def reduce_kernel(
    pages, tensors, kp, vp, wk, wv, out_ref,
    own, stage, from_core, page_stage, from_page, chip_stage, from_chip,
    core_send, core_recv, page_send, page_recv, chip_send, chip_recv,
):
    page, tensor, core, sibling = place()
    chips = tensors // 2
    chip = tensor // 2
    rows, width = out_ref.shape
    nt = (((1,), (1,)), ((), ()))
    wait_barrier = greet(pages, tensors)
    def partial(slots, group):
        take = pl.ds(pl.multiple_of(group * width, width), width)

        def rows_of(piece):
            return jnp.concatenate([piece[slot * rows : (slot + 1) * rows] for slot in slots], axis=0)

        product = lax.dot_general(rows_of(kp), wk[take], nt, preferred_element_type=F32) + lax.dot_general(
            rows_of(vp), wv[take], nt, preferred_element_type=F32
        )
        return [product[i * rows : (i + 1) * rows] for i in range(len(slots))]

    def to_core(slot, there):
        return remote(
            stage.at[slot, there], from_core.at[slot, there], core_send.at[slot, there],
            core_recv.at[slot, there], {"tensor": sibling},
        )

    def to_page(side, there):
        return remote(
            page_stage.at[side, there], from_page.at[side, there], page_send.at[side, there],
            page_recv.at[side, there], {"page": page - 1 + 2 * side},
        )

    def to_chip(there):
        return remote(
            chip_stage.at[there], from_chip.at[chip], chip_send.at[there], chip_recv.at[chip],
            {"tensor": 2 * there + core},
        )

    def chip_arrived(there):
        remote(
            chip_stage.at[there], from_chip.at[there], chip_send.at[there], chip_recv.at[there],
            {"tensor": 2 * there + core},
        ).wait_recv()

    order = [lax.rem(chip + 1 + k, chips) for k in range(chips)]

    sides = (page > 0, page < pages - 1)

    def for_core(slots, there):
        for slot, product in zip(slots, partial(slots, 2 * there + 1 - core)):
            stage[slot, there] = product.astype(BF16)

    for there in order:
        for_core((0, 2), there)
        if there is order[0]:
            wait_barrier()
        for slot in (0, 2):
            to_core(slot, there).start()
        mine = partial((0, 2), 2 * there + core)
        for slot, product in zip((0, 2), mine):
            own[slot, there] = product
        for slot in (0, 2):
            to_core(slot, there).wait_recv()

            @pl.when(sides[slot // 2])
            def _():
                page_stage[slot // 2, there] = (own[slot, there] + from_core[slot, there].astype(F32)).astype(BF16)
                to_page(slot // 2, there).start()
    for there in order:
        for_core((1,), there)
        to_core(1, there).start()
    for there in order:
        own[1, there] = partial((1,), 2 * there + core)[0]
    for there in order:
        to_core(1, there).wait_recv()
        own[1, there] += from_core[1, there].astype(F32)
    for there in order:
        for side in (0, 1):
            @pl.when(sides[1 - side])
            def _():
                to_page(side, there).wait_recv()
                own[1, there] += from_page[side, there].astype(F32)

        if there is not order[-1]:
            chip_stage[there] = own[1, there].astype(BF16)
            to_chip(there).start()
    total = own[1, chip]
    for there in order[:-1]:
        chip_arrived(there)
        total = total + from_chip[there].astype(F32)
    out_ref[...] = total.astype(BF16)
    for there in order:
        for slot in range(3):
            to_core(slot, there).wait_send()
        for side in (0, 1):
            @pl.when(sides[side])
            def _():
                to_page(side, there).wait_send()

        if there is not order[-1]:
            to_chip(there).wait_send()


def on_device(pages, tensors, query, memory, key_weight, value_weight, out_grad, mask_blocks):
    tokens, features = query.shape
    rows, width = memory.shape
    depth = key_weight.shape[0]
    chips = tensors // 2
    in_vmem = pl.BlockSpec(memory_space=pltpu.VMEM)
    in_hbm = pl.BlockSpec(memory_space=pltpu.HBM)
    dma = pltpu.SemaphoreType.DMA
    keys, values = pl.pallas_call(
        functools.partial(project_kernel, pages, tensors),
        out_shape=[jax.ShapeDtypeStruct((3 * rows, features), BF16)] * 2,
        in_specs=[in_hbm] * 3,
        out_specs=[in_vmem, in_vmem],
        scratch_shapes=[
            pltpu.VMEM((3, tensors, rows, width), BF16),
            pltpu.VMEM((depth, features), BF16),
            pltpu.VMEM((depth, features), BF16),
            dma((3,)),
            dma((6, tensors, HALVES)),
            dma((3, tensors, HALVES)),
        ],
        compiler_params=pltpu.CompilerParams(
            collective_id=0, has_side_effects=True, vmem_limit_bytes=GATHER_LIMIT
        ),
        name="gather_project",
    )(*[pltpu.with_memory_space_constraint(a, pltpu.HBM) for a in (memory, key_weight, value_weight)])

    heads = 2
    step = heads * HD
    column = lambda i: (0, i)
    attended, query_grad, key_piece, value_piece = pl.pallas_call(
        functools.partial(attend_kernel, pages),
        grid=(features // step,),
        out_shape=[jax.ShapeDtypeStruct((tokens, features), BF16)] * 2
        + [jax.ShapeDtypeStruct((3 * rows, features), BF16)] * 2,
        in_specs=[
            pl.BlockSpec(memory_space=pltpu.SMEM),
            pl.BlockSpec((tokens, step), column),
            pl.BlockSpec((tokens, step), column),
            pl.BlockSpec((3 * rows, step), column),
            pl.BlockSpec((3 * rows, step), column),
        ],
        out_specs=[
            pl.BlockSpec((tokens, step), column),
            pl.BlockSpec((tokens, step), column),
            pl.BlockSpec((3 * rows, step), column),
            pl.BlockSpec((3 * rows, step), column),
        ],
        compiler_params=pltpu.CompilerParams(vmem_limit_bytes=VMEM_LIMIT),
        name="attend",
    )(jnp.swapaxes(mask_blocks, 2, 3), query, out_grad, keys, values)

    memory_grad = pl.pallas_call(
        functools.partial(reduce_kernel, pages, tensors),
        out_shape=jax.ShapeDtypeStruct((rows, width), BF16),
        in_specs=[in_vmem] * 4,
        out_specs=in_vmem,
        scratch_shapes=[
            pltpu.VMEM((3, chips, rows, width), F32),
            pltpu.VMEM((3, chips, rows, width), BF16),
            pltpu.VMEM((3, chips, rows, width), BF16),
            pltpu.VMEM((2, chips, rows, width), BF16),
            pltpu.VMEM((2, chips, rows, width), BF16),
            pltpu.VMEM((chips, rows, width), BF16),
            pltpu.VMEM((chips, rows, width), BF16),
            dma((3, chips)),
            dma((3, chips)),
            dma((2, chips)),
            dma((2, chips)),
            dma((chips,)),
            dma((chips,)),
        ],
        compiler_params=pltpu.CompilerParams(
            collective_id=1, has_side_effects=True, vmem_limit_bytes=VMEM_LIMIT
        ),
        name="back_project_reduce",
    )(key_piece, value_piece, key_weight, value_weight)
    return attended, query_grad, memory_grad


def solution(mesh):
    placed = (
        P(("groups", "page"), "tensor"),
        P(("groups", "page"), "tensor"),
        P(None, "tensor"),
        P(None, "tensor"),
        P(("groups", "page"), "tensor"),
        P(("groups", "page"), None, None, None),
    )
    return jax.shard_map(
        functools.partial(on_device, mesh.shape["page"], mesh.shape["tensor"]),
        mesh=mesh,
        in_specs=placed,
        out_specs=(
            P(("groups", "page"), "tensor"),
            P(("groups", "page"), "tensor"),
            P(("groups", "page"), "tensor"),
        ),
        check_vma=False,
    )
```

```python
import functools
import math

import jax
import jax.numpy as jnp
from jax import lax
from jax.experimental import pallas as pl
from jax.experimental.pallas import tpu as pltpu
from jax.sharding import PartitionSpec as P

HD = 128
HALVES = 1
MESH = pl.DeviceIdType.MESH
VMEM_LIMIT = 24 * 1024 * 1024
GATHER_LIMIT = 24 * 1024 * 1024
F32 = jnp.float32
BF16 = jnp.bfloat16


def place():
    page = lax.axis_index("page")
    tensor = lax.axis_index("tensor")
    core = lax.rem(tensor, 2)
    return page, tensor, core, tensor + 1 - 2 * core


def greet(pages, tensors):
    page, tensor, core, sibling = place()
    barrier = pltpu.get_barrier_semaphore()
    chips = tensors // 2

    def signal(where):
        pl.semaphore_signal(barrier, inc=1, device_id=where, device_id_type=MESH)

    signal({"tensor": sibling})
    for d in range(1, chips):
        signal({"tensor": lax.rem(tensor + 2 * d, tensors)})

    @pl.when(page > 0)
    def _():
        signal({"page": page - 1})

    @pl.when(page < pages - 1)
    def _():
        signal({"page": page + 1})

    def wait():
        at_end = jnp.where(page > 0, 1, 0) + jnp.where(page < pages - 1, 1, 0)
        pl.semaphore_wait(barrier, chips + at_end)

    return wait


def remote(src, dst, send, recv, where):
    return pltpu.make_async_remote_copy(
        src_ref=src, dst_ref=dst, send_sem=send, recv_sem=recv, device_id=where, device_id_type=MESH
    )


def project_kernel(
    pages, tensors, mem_ref, wk_hbm, wv_hbm, keys, values,
    gathered, wk, wv, load_sem, send_sem, recv_sem,
):
    page, tensor, core, sibling = place()
    chips = tensors // 2
    rows, width = mem_ref.shape
    features = wk.shape[1]
    tile = min(256, features)

    loads = [
        pltpu.make_async_copy(mem_ref, gathered.at[1, tensor], load_sem.at[2]),
        pltpu.make_async_copy(wk_hbm, wk, load_sem.at[0]),
        pltpu.make_async_copy(wv_hbm, wv, load_sem.at[1]),
    ]
    wait_barrier = greet(pages, tensors)
    for load in loads:
        load.start()
    has_prev = page > 0
    has_next = page < pages - 1

    half = rows // HALVES

    def part(ref, h):
        return ref.at[pl.ds(h * half, half)]

    def shard(slot, owner, h):
        return gathered.at[slot, owner, pl.ds(h * half, half)]

    def to_sibling(src, slot, owner, h):
        return remote(src, shard(slot, owner, h), send_sem.at[slot, owner, h], recv_sem.at[slot, owner, h], {"tensor": sibling})

    def to_chip(d, h):
        there = lax.rem(tensor + 2 * d, tensors)
        return remote(part(mem_ref, h), shard(1, tensor, h), send_sem.at[3, there, h], recv_sem.at[1, tensor, h], {"tensor": there})

    def to_next(src, owner, h):
        return remote(src, shard(0, owner, h), send_sem.at[4, owner, h], recv_sem.at[0, owner, h], {"page": page + 1})

    def to_prev(src, owner, h):
        return remote(src, shard(2, owner, h), send_sem.at[5, owner, h], recv_sem.at[2, owner, h], {"page": page - 1})

    def arrived(slot, owner, h):
        here = shard(slot, owner, h)
        remote(here, here, send_sem.at[0, owner, h], recv_sem.at[slot, owner, h], {"tensor": sibling}).wait_recv()

    def spread(src, owner, h):
        @pl.when(has_next)
        def _():
            to_next(src, owner, h).start()

        @pl.when(has_prev)
        def _():
            to_prev(src, owner, h).start()

    wait_barrier()
    for h in range(HALVES):
        for d in range(1, chips):
            to_chip(d, h).start()
        spread(part(mem_ref, h), tensor, h)
    for h in range(HALVES):
        to_sibling(part(mem_ref, h), 1, tensor, h).start()
    peers = [lax.rem(tensor + 2 * d, tensors) for d in range(chips)]
    for owner in peers[1:]:
        for h in range(HALVES):
            arrived(1, owner, h)
            spread(shard(1, owner, h), owner, h)
            to_sibling(shard(1, owner, h), 1, owner, h).start()

    def project(slots):
        def step(i, _):
            columns = pl.ds(pl.multiple_of(i * tile, tile), tile)
            whole = jnp.concatenate(
                [
                    jnp.concatenate([gathered[slot, owner] for owner in range(tensors)], axis=1)
                    for slot in slots
                ],
                axis=0,
            )
            for weight, out in ((wk, keys), (wv, values)):
                product = jnp.dot(whole, weight[:, columns], preferred_element_type=F32).astype(BF16)
                for j, slot in enumerate(slots):
                    out[slot * rows : (slot + 1) * rows, columns] = product[j * rows : (j + 1) * rows]
            return 0

        lax.fori_loop(0, features // tile, step, 0)

    def other(owner):
        return owner + 1 - 2 * lax.rem(owner, 2)

    def pass_on(owner, h):
        for slot, there in ((0, has_prev), (2, has_next)):
            @pl.when(there)
            def _():
                arrived(slot, owner, h)
                to_sibling(shard(slot, owner, h), slot, owner, h).start()

    for owner in peers:
        for h in range(HALVES):
            arrived(1, other(owner), h)
    for load in loads:
        load.wait()
    project((1,))
    for owner in peers:
        for h in range(HALVES):
            pass_on(owner, h)
    for slot, there in ((0, has_prev), (2, has_next)):
        @pl.when(there)
        def _():
            for owner in peers:
                for h in range(HALVES):
                    arrived(slot, other(owner), h)

        @pl.when(jnp.logical_not(there))
        def _():
            gathered[slot] = jnp.zeros(gathered.shape[1:], BF16)

    project((0, 2))
    for h in range(HALVES):
        for d in range(1, chips):
            to_chip(d, h).wait_send()
        for owner in peers:
            src = part(mem_ref, h)
            to_sibling(src, 1, owner, h).wait_send()

            @pl.when(has_next)
            def _():
                to_next(src, owner, h).wait_send()
                to_sibling(src, 2, owner, h).wait_send()

            @pl.when(has_prev)
            def _():
                to_prev(src, owner, h).wait_send()
                to_sibling(src, 0, owner, h).wait_send()


def attend_kernel(pages, mask_ref, q_ref, g_ref, k_ref, v_ref, att_ref, qg_ref, kp_ref, vp_ref):
    page = lax.axis_index("page")
    slots, memory_blocks, query_blocks = mask_ref.shape[1:]
    block = q_ref.shape[0] // query_blocks
    scale = 1.0 / math.sqrt(HD)
    rate = scale * math.log2(math.e)
    nt = (((1,), (1,)), ((), ()))
    tn = (((0,), (0,)), ((), ()))
    heads = q_ref.shape[1] // HD
    bias = {}
    for slot in range(slots):
        source = page + (slot - 1)
        live = jnp.logical_and(source >= 0, source < pages)
        for tb in range(query_blocks):
            for mb in range(memory_blocks):
                seen = jnp.logical_and(mask_ref[0, slot, mb, tb] > 0, live)
                bias[tb, slot * memory_blocks + mb] = jnp.where(seen, 0.0, -1e30).astype(F32)

    def columns(head):
        return slice(head * HD, (head + 1) * HD)

    def products(head):
        cols = columns(head)
        return (
            lax.dot_general(k_ref[:, cols], q_ref[:, cols], nt, preferred_element_type=F32),
            lax.dot_general(v_ref[:, cols], g_ref[:, cols], nt, preferred_element_type=F32),
        )

    def softmax(scores, weight_grad):
        rounded, score_grads = [], []
        for tb in range(query_blocks):
            span = slice(tb * block, (tb + 1) * block)
            biased = jnp.concatenate(
                [
                    scores[i * block : (i + 1) * block, span] + bias[tb, i]
                    for i in range(slots * memory_blocks)
                ],
                axis=0,
            )
            top = jnp.max(biased, axis=0, keepdims=True)
            exponent = jnp.exp2((biased - top) * rate)
            weights = exponent * (1.0 / jnp.sum(exponent, axis=0, keepdims=True))
            rounded.append(weights.astype(BF16))
            grad = weight_grad[:, span]
            inner = jnp.sum(weights * grad, axis=0, keepdims=True)
            score_grads.append((weights * (grad - inner)).astype(BF16))
        return jnp.concatenate(rounded, axis=1), jnp.concatenate(score_grads, axis=1)

    def outputs(head, rounded, score_grad):
        cols = columns(head)
        att = lax.dot_general(v_ref[:, cols], rounded, tn, preferred_element_type=F32)
        att_ref[:, cols] = att.T.astype(BF16)
        qg = lax.dot_general(k_ref[:, cols], score_grad, tn, preferred_element_type=F32) * scale
        qg_ref[:, cols] = qg.T.astype(BF16)
        vp_ref[:, cols] = jnp.dot(rounded, g_ref[:, cols], preferred_element_type=F32).astype(BF16)
        kp = jnp.dot(score_grad, q_ref[:, cols], preferred_element_type=F32) * scale
        kp_ref[:, cols] = kp.astype(BF16)

    ahead, ready = products(0), None
    for head in range(heads):
        now = ahead
        if head + 1 < heads:
            ahead = products(head + 1)
        done = softmax(*now)
        if ready is not None:
            outputs(head - 1, *ready)
        ready = done
    outputs(heads - 1, *ready)


def reduce_kernel(
    pages, tensors, kp, vp, wk, wv, out_ref,
    own, stage, from_core, page_stage, from_page, chip_stage, from_chip,
    core_send, core_recv, page_send, page_recv, chip_send, chip_recv,
):
    page, tensor, core, sibling = place()
    chips = tensors // 2
    chip = tensor // 2
    rows, width = out_ref.shape
    nt = (((1,), (1,)), ((), ()))
    wait_barrier = greet(pages, tensors)
    def partial(slots, group):
        take = pl.ds(pl.multiple_of(group * width, width), width)

        def rows_of(piece):
            return jnp.concatenate([piece[slot * rows : (slot + 1) * rows] for slot in slots], axis=0)

        product = lax.dot_general(rows_of(kp), wk[take], nt, preferred_element_type=F32) + lax.dot_general(
            rows_of(vp), wv[take], nt, preferred_element_type=F32
        )
        return [product[i * rows : (i + 1) * rows] for i in range(len(slots))]

    def to_core(slot, there):
        return remote(
            stage.at[slot, there], from_core.at[slot, there], core_send.at[slot, there],
            core_recv.at[slot, there], {"tensor": sibling},
        )

    def to_page(side, there):
        return remote(
            page_stage.at[side, there], from_page.at[side, there], page_send.at[side, there],
            page_recv.at[side, there], {"page": page - 1 + 2 * side},
        )

    def to_chip(there):
        return remote(
            chip_stage.at[there], from_chip.at[chip], chip_send.at[there], chip_recv.at[chip],
            {"tensor": 2 * there + core},
        )

    def chip_arrived(there):
        remote(
            chip_stage.at[there], from_chip.at[there], chip_send.at[there], chip_recv.at[there],
            {"tensor": 2 * there + core},
        ).wait_recv()

    order = [lax.rem(chip + 1 + k, chips) for k in range(chips)]

    sides = (page > 0, page < pages - 1)

    def for_core(slots, there):
        for slot, product in zip(slots, partial(slots, 2 * there + 1 - core)):
            stage[slot, there] = product.astype(BF16)

    for there in order:
        for_core((0, 2), there)
        if there is order[0]:
            wait_barrier()
        for slot in (0, 2):
            to_core(slot, there).start()
        mine = partial((0, 2), 2 * there + core)
        for slot, product in zip((0, 2), mine):
            own[slot, there] = product
        for slot in (0, 2):
            to_core(slot, there).wait_recv()

            @pl.when(sides[slot // 2])
            def _():
                page_stage[slot // 2, there] = (own[slot, there] + from_core[slot, there].astype(F32)).astype(BF16)
                to_page(slot // 2, there).start()
    for there in order:
        for_core((1,), there)
        to_core(1, there).start()
    for there in order:
        own[1, there] = partial((1,), 2 * there + core)[0]
    for there in order:
        to_core(1, there).wait_recv()
        own[1, there] += from_core[1, there].astype(F32)
    for there in order:
        for side in (0, 1):
            @pl.when(sides[1 - side])
            def _():
                to_page(side, there).wait_recv()
                own[1, there] += from_page[side, there].astype(F32)

        if there is not order[-1]:
            chip_stage[there] = own[1, there].astype(BF16)
            to_chip(there).start()
    total = own[1, chip]
    for there in order[:-1]:
        chip_arrived(there)
        total = total + from_chip[there].astype(F32)
    out_ref[...] = total.astype(BF16)
    for there in order:
        for slot in range(3):
            to_core(slot, there).wait_send()
        for side in (0, 1):
            @pl.when(sides[side])
            def _():
                to_page(side, there).wait_send()

        if there is not order[-1]:
            to_chip(there).wait_send()


def on_device(pages, tensors, query, memory, key_weight, value_weight, out_grad, mask_blocks):
    tokens, features = query.shape
    rows, width = memory.shape
    depth = key_weight.shape[0]
    chips = tensors // 2
    in_vmem = pl.BlockSpec(memory_space=pltpu.VMEM)
    in_hbm = pl.BlockSpec(memory_space=pltpu.HBM)
    dma = pltpu.SemaphoreType.DMA
    keys, values = pl.pallas_call(
        functools.partial(project_kernel, pages, tensors),
        out_shape=[jax.ShapeDtypeStruct((3 * rows, features), BF16)] * 2,
        in_specs=[in_hbm] * 3,
        out_specs=[in_vmem, in_vmem],
        scratch_shapes=[
            pltpu.VMEM((3, tensors, rows, width), BF16),
            pltpu.VMEM((depth, features), BF16),
            pltpu.VMEM((depth, features), BF16),
            dma((3,)),
            dma((6, tensors, HALVES)),
            dma((3, tensors, HALVES)),
        ],
        compiler_params=pltpu.CompilerParams(
            collective_id=0, has_side_effects=True, vmem_limit_bytes=GATHER_LIMIT
        ),
        name="gather_project",
    )(*[pltpu.with_memory_space_constraint(a, pltpu.HBM) for a in (memory, key_weight, value_weight)])

    heads = 2
    step = heads * HD
    column = lambda i: (0, i)
    attended, query_grad, key_piece, value_piece = pl.pallas_call(
        functools.partial(attend_kernel, pages),
        grid=(features // step,),
        out_shape=[jax.ShapeDtypeStruct((tokens, features), BF16)] * 2
        + [jax.ShapeDtypeStruct((3 * rows, features), BF16)] * 2,
        in_specs=[
            pl.BlockSpec(memory_space=pltpu.SMEM),
            pl.BlockSpec((tokens, step), column),
            pl.BlockSpec((tokens, step), column),
            pl.BlockSpec((3 * rows, step), column),
            pl.BlockSpec((3 * rows, step), column),
        ],
        out_specs=[
            pl.BlockSpec((tokens, step), column),
            pl.BlockSpec((tokens, step), column),
            pl.BlockSpec((3 * rows, step), column),
            pl.BlockSpec((3 * rows, step), column),
        ],
        compiler_params=pltpu.CompilerParams(vmem_limit_bytes=VMEM_LIMIT),
        name="attend",
    )(jnp.swapaxes(mask_blocks, 2, 3), query, out_grad, keys, values)

    memory_grad = pl.pallas_call(
        functools.partial(reduce_kernel, pages, tensors),
        out_shape=jax.ShapeDtypeStruct((rows, width), BF16),
        in_specs=[in_vmem] * 4,
        out_specs=in_vmem,
        scratch_shapes=[
            pltpu.VMEM((3, chips, rows, width), F32),
            pltpu.VMEM((3, chips, rows, width), BF16),
            pltpu.VMEM((3, chips, rows, width), BF16),
            pltpu.VMEM((2, chips, rows, width), BF16),
            pltpu.VMEM((2, chips, rows, width), BF16),
            pltpu.VMEM((chips, rows, width), BF16),
            pltpu.VMEM((chips, rows, width), BF16),
            dma((3, chips)),
            dma((3, chips)),
            dma((2, chips)),
            dma((2, chips)),
            dma((chips,)),
            dma((chips,)),
        ],
        compiler_params=pltpu.CompilerParams(
            collective_id=1, has_side_effects=True, vmem_limit_bytes=VMEM_LIMIT
        ),
        name="back_project_reduce",
    )(key_piece, value_piece, key_weight, value_weight)
    return attended, query_grad, memory_grad


def solution(mesh):
    placed = (
        P(("groups", "page"), "tensor"),
        P(("groups", "page"), "tensor"),
        P(None, "tensor"),
        P(None, "tensor"),
        P(("groups", "page"), "tensor"),
        P(("groups", "page"), None, None, None),
    )
    return jax.shard_map(
        functools.partial(on_device, mesh.shape["page"], mesh.shape["tensor"]),
        mesh=mesh,
        in_specs=placed,
        out_specs=(
            P(("groups", "page"), "tensor"),
            P(("groups", "page"), "tensor"),
            P(("groups", "page"), "tensor"),
        ),
        check_vma=False,
    )
```
